32 devices in a mesh: groups: 2 (over x), row: 16 (over z, y, core).
Axes of the slice: x: 2, y: 2, z: 4, core: 2. Of those that a mesh axis runs over, the one named last changes fastest.
Arguments:
- gated_hidden_rows: bfloat16 [2, 384, 28672], P(None, 'groups', 'row'), parts along dimension 1, may hold values from -6 to 6
- down_base_weight: bfloat16 [8192, 28672], P('row'), may hold values from -0.03125 to 0.03125
- adapter_input_factor: bfloat16 [8, 64, 28672], P(None, None, 'row'), may hold values from -0.03125 to 0.03125
- adapter_output_weight: bfloat16 [8, 64, 8192], P(None, None, 'row'), may hold values from -0.75 to 0.75
- request_adapter_index: int32 [2, 384], P(None, 'groups'), parts along dimension 1, may hold values from 0 to 7, as said below
Outputs:
- ffn_out: bfloat16 [2, 384, 8192], P(None, 'groups', 'row'), parts along dimension 1
The draws below stay inside these ranges and needn't reach their ends.
There are 2 independent parts, one for each index of `groups`. The reference program is written for one: setup_inputs(seed, part) draws one part's arguments, and reference() takes and returns one part's arrays. A program takes and returns all parts, laid end to end along the dimension named above; an argument that names none is the same for every part. Nothing has to cross between parts.
Inputs may be any that keep to these rules, and one draw needn't show every extreme that they name: `request_adapter_index`: each entry names one of the 8 adapters; adapter 0 is the resident adapter that is merged into the weights.
All inputs are finite; a program needn't handle non-finite values.
Results may differ from the reference program's by a relative error of at most 0.0038.
Values may be sent and summed in bfloat16 or wider, within the bound.
A program may use at most 128 MiB of HBM per device.

```python
import jax
import jax.numpy as jnp
from jax import lax

MODEL_WIDTH = 8192
HIDDEN_UNITS = 28672
ADAPTER_RANK = 64
ADAPTER_COUNT = 8
ROWS = 192
STEPS = 2


def draw_request_adapter_index(key, part):
    picks = jax.random.randint(key, (STEPS, ROWS), 0, 2 * ADAPTER_COUNT - 2)
    return jnp.where(picks < ADAPTER_COUNT - 1, picks + 1, 0).astype(jnp.int32)


def block_scale(key, dims, split, smallest, top_value):
    factor_of, own = 1.0, jax.random.fold_in(key, 6)
    for axis_at, blocks in split:
        draws = jnp.exp(jax.random.uniform(jax.random.fold_in(own, axis_at), (blocks,), jnp.float32, smallest / len(split), top_value / len(split)))
        factor_of = factor_of * jnp.repeat(draws, dims[axis_at] // blocks).reshape([-1 if axis == axis_at else 1 for axis in range(len(dims))])
    return factor_of


def gaussian(own_key, shape, scale, bound, cuts=(), kind=jnp.bfloat16):
    drawn = jax.random.normal(own_key, shape, jnp.float32) * scale
    if len(cuts) > 0:
        drawn = block_scale(own_key, shape, cuts, -0.22, 0.18) * drawn
    return jnp.clip(drawn, min=-bound, max=bound).astype(kind)


def setup_inputs(seed: int = 0, part: int = 0) -> dict:
    splits = jax.random.split(jax.random.key(seed), 6)
    own_keys = jax.random.split(jax.random.fold_in(splits[5], part), 6)
    gated_hidden_rows = gaussian(own_keys[0], (STEPS, ROWS, HIDDEN_UNITS), 1.0, 6.0, ((2, 16),))
    down_base_weight = gaussian(splits[1], (MODEL_WIDTH, HIDDEN_UNITS), HIDDEN_UNITS ** -0.5, 0.03125, ((0, 16),))
    adapter_input_factor = gaussian(splits[2], (ADAPTER_COUNT, ADAPTER_RANK, HIDDEN_UNITS), HIDDEN_UNITS ** -0.5, 0.03125, ((2, 16),))
    adapter_output_weight = gaussian(splits[3], (ADAPTER_COUNT, ADAPTER_RANK, MODEL_WIDTH), ADAPTER_RANK ** -0.5, 0.75, ((2, 16),))
    request_adapter_index = draw_request_adapter_index(jax.random.fold_in(jax.random.fold_in(splits[5], part), 71), part)
    return dict(gated_hidden_rows=gated_hidden_rows, down_base_weight=down_base_weight, adapter_input_factor=adapter_input_factor, adapter_output_weight=adapter_output_weight, request_adapter_index=request_adapter_index)


def select_pair(project_rows, adapter_labels, request_count, rank_index):
    choose = (adapter_labels[:, None] == jnp.arange(request_count, dtype=jnp.int32)[None, :]).astype(jnp.float32)
    total = project_rows.shape[0]
    own = jnp.sum(project_rows.reshape(total, request_count, rank_index) * choose[:, :, None], axis=1)
    resident_weight = project_rows[:, :rank_index]
    keep = (adapter_labels != 0).astype(jnp.float32)[:, None]
    return jnp.concatenate([own, resident_weight], axis=1) * keep


def expand_factor(shrunk_rows, adapter_labels, adapter_output_weight):
    request_count = adapter_output_weight.shape[0]
    rank_index = adapter_output_weight.shape[1]
    total = shrunk_rows.shape[0]
    choose = (adapter_labels[:, None] == jnp.arange(request_count, dtype=jnp.int32)[None, :]).astype(jnp.float32)
    spread = (choose[:, :, None] * shrunk_rows[:, None, :rank_index].astype(jnp.float32)).reshape(total, request_count * rank_index)
    operand = jnp.concatenate([spread.astype(jnp.bfloat16), shrunk_rows[:, rank_index:]], axis=1)
    stacked_weights = jnp.concatenate([adapter_output_weight.reshape(request_count * rank_index, adapter_output_weight.shape[2]), -adapter_output_weight[0]], axis=0)
    return jnp.dot(operand, stacked_weights, preferred_element_type=jnp.float32)


def reference(gated_hidden_rows, down_base_weight, adapter_input_factor, adapter_output_weight, request_adapter_index):
    merged_weight = down_base_weight.astype(jnp.float32) + jnp.dot(adapter_output_weight[0].T, adapter_input_factor[0], preferred_element_type=jnp.float32)
    flattened_rows = gated_hidden_rows.reshape(STEPS * ROWS, HIDDEN_UNITS)
    adapter_labels = request_adapter_index.reshape(STEPS * ROWS)
    base = jnp.dot(flattened_rows.astype(jnp.float32), merged_weight.T, precision=lax.Precision.HIGHEST)
    project_rows = jnp.dot(flattened_rows, adapter_input_factor.reshape(ADAPTER_COUNT * ADAPTER_RANK, HIDDEN_UNITS).T, preferred_element_type=jnp.float32)
    shrunk_rows = select_pair(project_rows, adapter_labels, ADAPTER_COUNT, ADAPTER_RANK).astype(jnp.bfloat16)
    adapter_update = expand_factor(shrunk_rows, adapter_labels, adapter_output_weight)
    return (base + adapter_update).astype(jnp.bfloat16).reshape(STEPS, ROWS, MODEL_WIDTH)
```

```python
import functools

import jax
import jax.numpy as jnp
from jax import lax
from jax.experimental import pallas as pl
from jax.experimental.pallas import tpu as pltpu
from jax.sharding import PartitionSpec as P

CONTRACT = (((1,), (1,)), ((), ()))


def select_both(project_rows, adapter_labels, request_count, rank_index):
    choose = (
        adapter_labels[:, None] == jnp.arange(request_count, dtype=jnp.int32)[None, :]
    ).astype(jnp.float32)
    total = project_rows.shape[0]
    own = jnp.sum(
        project_rows.reshape(total, request_count, rank_index) * choose[:, :, None], axis=1
    )
    return jnp.concatenate([own, project_rows[:, :rank_index]], axis=1)


def expand_factor(shrunk_rows, adapter_labels, adapter_output_weight):
    request_count = adapter_output_weight.shape[0]
    rank_index = adapter_output_weight.shape[1]
    total = shrunk_rows.shape[0]
    choose = (
        adapter_labels[:, None] == jnp.arange(request_count, dtype=jnp.int32)[None, :]
    ).astype(jnp.float32)
    spread = (choose[:, :, None] * shrunk_rows[:, None, :rank_index].astype(jnp.float32)).reshape(
        total, request_count * rank_index
    )
    operand = jnp.concatenate([spread.astype(jnp.bfloat16), shrunk_rows[:, rank_index:]], axis=1)
    stacked_weights = jnp.concatenate(
        [
            adapter_output_weight.reshape(
                request_count * rank_index, adapter_output_weight.shape[2]
            ),
            -adapter_output_weight[0],
        ],
        axis=0,
    )
    return jnp.dot(operand, stacked_weights, preferred_element_type=jnp.float32)


def gather_kernel(Z, NA, CH, x_ref, w_ref, out_ref, hbuf, wbuf, xsem, wsem, rsem, ssem):
    n = 4 * Z
    me = lax.axis_index("row")
    c = lax.rem(me, 2)
    y = lax.rem(me // 2, 2)
    z = me // 4
    units = x_ref.shape[1]
    RIGHT, LEFT, ACROSS, TWIN = 0, 1, 2, 3

    def blk(zz, yy, cc):
        return (zz * 2 + yy) * 2 + cc

    target = (
        blk(jnp.minimum(z + 1, Z - 1), y, c),
        blk(jnp.maximum(z - 1, 0), y, c),
        blk(z, 1 - y, c),
        blk(z, y, 1 - c),
    )
    has_right, has_left = z < Z - 1, z > 0

    def remote(k, j, way):
        rows = pl.ds(pl.multiple_of(j * CH, CH), CH)
        return pltpu.make_async_remote_copy(
            src_ref=hbuf.at[k, rows],
            dst_ref=hbuf.at[k, rows],
            send_sem=ssem.at[way, k // 2, j],
            recv_sem=rsem.at[k, j],
            device_id={"row": target[way]},
            device_id_type=pl.DeviceIdType.MESH,
        )

    def arrived(k, j):
        remote(k, j, TWIN).wait_recv()

    def weight(k):
        cols = pl.ds(pl.multiple_of(k * units, 128), units)
        return pltpu.make_async_copy(w_ref.at[:, cols], wbuf.at[k], wsem.at[k])

    own = pltpu.make_async_copy(x_ref, hbuf.at[me], xsem)
    own.start()

    barrier = pltpu.get_barrier_semaphore()

    def greet(dev):
        pl.semaphore_signal(
            barrier, inc=1, device_id={"row": dev}, device_id_type=pl.DeviceIdType.MESH
        )

    greet(target[ACROSS])
    greet(target[TWIN])

    @pl.when(has_right)
    def _():
        greet(target[RIGHT])

    @pl.when(has_left)
    def _():
        greet(target[LEFT])

    pl.semaphore_wait(barrier, 2 + has_right.astype(jnp.int32) + has_left.astype(jnp.int32))
    own.wait()

    def go_right(k, j):
        @pl.when(has_right)
        def _():
            remote(k, j, RIGHT).start()

    def go_left(k, j):
        @pl.when(has_left)
        def _():
            remote(k, j, LEFT).start()

    remote(me, NA, ACROSS).start()

    @pl.loop(0, NA)
    def _(j):
        go_right(me, j)
        go_left(me, j)
        remote(me, j, ACROSS).start()
        remote(me, j, TWIN).start()

    go_right(me, NA)
    go_left(me, NA)
    remote(me, NA, TWIN).start()

    @pl.loop(0, n)
    def _(k):
        weight(k).start()

    out_ref[...] = jnp.zeros_like(out_ref)

    def from_left(k, j, across):
        arrived(k, j)
        go_right(k, j)
        if across:
            remote(k, j, ACROSS).start()
        remote(k, j, TWIN).start()

    def from_right(k, j, across):
        arrived(k, j)
        go_left(k, j)
        if across:
            remote(k, j, ACROSS).start()
        remote(k, j, TWIN).start()

    @pl.loop(1, Z + 2)
    def _(d):
        zl, zr = z - d, z + d
        yl, yr = z - (d - 1), z + (d - 1)

        @pl.when(d == 1)
        def _():
            k = blk(z, 1 - y, c)
            arrived(k, NA)
            go_right(k, NA)
            go_left(k, NA)
            remote(k, NA, TWIN).start()

        @pl.loop(0, 8)
        def _(j):
            @pl.when(j < NA)
            def _():
                @pl.when(zl >= 0)
                def _():
                    from_left(blk(zl, y, c), j, True)

                @pl.when(zr < Z)
                def _():
                    from_right(blk(zr, y, c), j, True)

                @pl.when(yl >= 0)
                def _():
                    k = blk(yl, 1 - y, c)
                    arrived(k, j)
                    remote(k, j, TWIN).start()

                @pl.when((yr < Z) & (d > 1))
                def _():
                    k = blk(yr, 1 - y, c)
                    arrived(k, j)
                    remote(k, j, TWIN).start()

            @pl.when((j == NA) | (j == NA + 1))
            def _():
                yy = jnp.where(j == NA, y, 1 - y)

                @pl.when(zl >= 0)
                def _():
                    from_left(blk(zl, yy, c), NA, False)

                @pl.when(zr < Z)
                def _():
                    from_right(blk(zr, yy, c), NA, False)

            e = d - 1
            twin, kind = j // 4, lax.rem(j, 4)
            crossed, up = kind // 2, lax.rem(kind, 2)
            dist = e - crossed
            zz = jnp.where(up == 1, z + dist, z - dist)
            valid = (dist >= 0) & (zz >= 0) & (zz < Z) & ((up == 0) | (dist > 0))

            @pl.when(valid)
            def _():
                k = blk(zz, jnp.where(crossed == 1, 1 - y, y), jnp.where(twin == 1, 1 - c, c))

                @pl.when(twin == 1)
                def _():
                    @pl.loop(0, NA + 1)
                    def _(i):
                        arrived(k, i)

                weight(k).wait()
                out_ref[...] += lax.dot_general(
                    hbuf[k], wbuf[k], CONTRACT, preferred_element_type=jnp.float32
                )

    @pl.loop(0, Z)
    def _(zz):
        @pl.loop(0, 2)
        def _(yy):
            k = blk(zz, yy, c)

            @pl.loop(0, NA + 1)
            def _(j):
                along = (yy == y) | (j == NA)

                @pl.when(has_right & (zz <= z) & along)
                def _():
                    remote(k, j, RIGHT).wait_send()

                @pl.when(has_left & (zz >= z) & along)
                def _():
                    remote(k, j, LEFT).wait_send()

                @pl.when((yy == y) & ((j < NA) | (zz == z)))
                def _():
                    remote(k, j, ACROSS).wait_send()

                remote(k, j, TWIN).wait_send()


def gathered_product(n, rows_in, weight):
    total, units = rows_in.shape
    features = weight.shape[0]
    parts = 6
    chunk = total // parts
    Z = n // 4
    return pl.pallas_call(
        functools.partial(gather_kernel, Z, parts - 1, chunk),
        out_shape=jax.ShapeDtypeStruct((total, features), jnp.float32),
        in_specs=[pl.BlockSpec(memory_space=pl.ANY)] * 2,
        out_specs=pl.BlockSpec(memory_space=pltpu.VMEM),
        scratch_shapes=[
            pltpu.VMEM((n, total, units), jnp.bfloat16),
            pltpu.VMEM((n, features, units), jnp.bfloat16),
            pltpu.SemaphoreType.DMA,
            pltpu.SemaphoreType.DMA((n,)),
            pltpu.SemaphoreType.DMA((n, parts)),
            pltpu.SemaphoreType.DMA((4, n // 2, parts)),
        ],
        compiler_params=pltpu.CompilerParams(
            collective_id=0, has_side_effects=True, vmem_limit_bytes=60 * 2**20
        ),
        cost_estimate=pl.CostEstimate(
            flops=2 * total * units * n * features,
            bytes_accessed=2 * n * units * (features + total),
            transcendentals=0,
        ),
    )(rows_in, weight)


def local(
    n,
    gated_hidden_rows,
    down_base_weight,
    adapter_input_factor,
    adapter_output_weight,
    request_adapter_index,
):
    steps, requests, device_units = gated_hidden_rows.shape
    request_count = adapter_input_factor.shape[0]
    rank_index = adapter_input_factor.shape[1]
    total = steps * requests
    flattened_rows = gated_hidden_rows.reshape(total, device_units)
    adapter_labels = request_adapter_index.reshape(total)
    project_rows = jnp.dot(
        flattened_rows,
        adapter_input_factor.reshape(request_count * rank_index, device_units).T,
        preferred_element_type=jnp.float32,
    )
    summand = select_both(project_rows, adapter_labels, request_count, rank_index)
    summed = lax.psum(summand, "row")
    keep = (adapter_labels != 0).astype(jnp.float32)[:, None]
    shrunk_rows = (summed * keep).astype(jnp.bfloat16)
    resident_sum = summed[:, rank_index:]
    highest = lax.Precision.HIGHEST
    fits = 2 * n * device_units * (total + down_base_weight.shape[0]) <= 54 * 2**20
    if n % 4 == 0 and device_units % 128 == 0 and total % 96 == 0 and fits:
        base = gathered_product(n, flattened_rows, down_base_weight)
    else:
        base = lax.dot_general(
            lax.all_gather(flattened_rows, "row", axis=1, tiled=True),
            down_base_weight,
            CONTRACT,
            preferred_element_type=jnp.float32,
        )
    base = base + jnp.dot(
        resident_sum, adapter_output_weight[0].astype(jnp.float32), precision=highest
    )
    adapter_update = expand_factor(shrunk_rows, adapter_labels, adapter_output_weight)
    return (base + adapter_update).astype(jnp.bfloat16).reshape(steps, requests, base.shape[1])


def solution(mesh):
    placed = (
        P(None, "groups", "row"),
        P("row", None),
        P(None, None, "row"),
        P(None, None, "row"),
        P(None, "groups"),
    )
    return jax.shard_map(
        functools.partial(local, mesh.shape["row"]),
        mesh=mesh,
        in_specs=placed,
        out_specs=P(None, "groups", "row"),
        check_vma=False,
    )
```

```python
import functools

import jax
import jax.numpy as jnp
from jax import lax
from jax.experimental import pallas as pl
from jax.experimental.pallas import tpu as pltpu
from jax.sharding import PartitionSpec as P

CONTRACT = (((1,), (1,)), ((), ()))


def select_both(project_rows, adapter_labels, request_count, rank_index):
    choose = (
        adapter_labels[:, None] == jnp.arange(request_count, dtype=jnp.int32)[None, :]
    ).astype(jnp.float32)
    total = project_rows.shape[0]
    own = jnp.sum(
        project_rows.reshape(total, request_count, rank_index) * choose[:, :, None], axis=1
    )
    return jnp.concatenate([own, project_rows[:, :rank_index]], axis=1)


def expand_factor(shrunk_rows, adapter_labels, adapter_output_weight):
    request_count = adapter_output_weight.shape[0]
    rank_index = adapter_output_weight.shape[1]
    total = shrunk_rows.shape[0]
    choose = (
        adapter_labels[:, None] == jnp.arange(request_count, dtype=jnp.int32)[None, :]
    ).astype(jnp.float32)
    spread = (choose[:, :, None] * shrunk_rows[:, None, :rank_index].astype(jnp.float32)).reshape(
        total, request_count * rank_index
    )
    operand = jnp.concatenate([spread.astype(jnp.bfloat16), shrunk_rows[:, rank_index:]], axis=1)
    stacked_weights = jnp.concatenate(
        [
            adapter_output_weight.reshape(
                request_count * rank_index, adapter_output_weight.shape[2]
            ),
            -adapter_output_weight[0],
        ],
        axis=0,
    )
    return jnp.dot(operand, stacked_weights, preferred_element_type=jnp.float32)


def served_kernel(
    Z,
    NA,
    CH,
    x_ref,
    w_ref,
    a_ref,
    b_ref,
    label_ref,
    out_ref,
    hbuf,
    wbuf,
    acc,
    labels,
    sums,
    totals,
    half_in,
    quarter_in,
    share_in,
    xsem,
    wsem,
    rsem,
    ssem,
    part_recv,
    part_send,
):
    n = 4 * Z
    me = lax.axis_index("row")
    c = lax.rem(me, 2)
    y = lax.rem(me // 2, 2)
    z = me // 4
    units = x_ref.shape[1]
    RIGHT, LEFT, ACROSS, TWIN = 0, 1, 2, 3

    def blk(zz, yy, cc):
        return (zz * 2 + yy) * 2 + cc

    target = (
        blk(jnp.minimum(z + 1, Z - 1), y, c),
        blk(jnp.maximum(z - 1, 0), y, c),
        blk(z, 1 - y, c),
        blk(z, y, 1 - c),
    )
    has_right, has_left = z < Z - 1, z > 0

    def remote(k, j, way):
        rows = pl.ds(pl.multiple_of(j * CH, CH), CH)
        return pltpu.make_async_remote_copy(
            src_ref=hbuf.at[k, rows],
            dst_ref=hbuf.at[k, rows],
            send_sem=ssem.at[way, k // 2, j],
            recv_sem=rsem.at[k, j],
            device_id={"row": target[way]},
            device_id_type=pl.DeviceIdType.MESH,
        )

    def arrived(k, j):
        remote(k, j, TWIN).wait_recv()

    def weight(k):
        cols = pl.ds(pl.multiple_of(k * units, 128), units)
        return pltpu.make_async_copy(w_ref.at[:, cols], wbuf.at[k], wsem.at[k])

    own = pltpu.make_async_copy(x_ref, hbuf.at[me], xsem)
    own.start()

    barrier = pltpu.get_barrier_semaphore()

    def greet(dev):
        pl.semaphore_signal(
            barrier, inc=1, device_id={"row": dev}, device_id_type=pl.DeviceIdType.MESH
        )

    greet(target[ACROSS])
    greet(target[TWIN])

    @pl.loop(0, Z)
    def _(zz):
        @pl.when(zz != z)
        def _():
            greet(blk(zz, y, c))

    pl.semaphore_wait(barrier, Z + 1)
    own.wait()

    def go_right(k, j):
        @pl.when(has_right)
        def _():
            remote(k, j, RIGHT).start()

    def go_left(k, j):
        @pl.when(has_left)
        def _():
            remote(k, j, LEFT).start()

    remote(me, NA, ACROSS).start()

    @pl.loop(0, NA)
    def _(j):
        go_right(me, j)
        go_left(me, j)
        remote(me, j, ACROSS).start()
        remote(me, j, TWIN).start()

    go_right(me, NA)
    go_left(me, NA)
    remote(me, NA, TWIN).start()

    @pl.loop(0, n)
    def _(k):
        weight(k).start()

    acc[...] = jnp.zeros_like(acc)

    total, lanes = sums.shape
    rank = lanes // 2
    steps, requests = label_ref.shape
    same = lax.broadcasted_iota(jnp.int32, (requests, requests), 0) == (
        lax.broadcasted_iota(jnp.int32, (requests, requests), 1)
    )
    for s in range(steps):
        row = label_ref[s : s + 1, :].astype(jnp.float32)
        column = jnp.sum(jnp.where(same, row, 0.0), axis=1, keepdims=True)
        labels[s * requests : (s + 1) * requests, :] = jnp.broadcast_to(column, (requests, lanes))

    width = a_ref.shape[0]
    adapter_of_lane = (lax.broadcasted_iota(jnp.int32, (1, width), 1) // rank).astype(jnp.float32)
    low = lax.broadcasted_iota(jnp.int32, (1, lanes), 1) < rank
    projected = lax.dot_general(
        hbuf[me], a_ref[...], CONTRACT, preferred_element_type=jnp.float32
    )
    chosen = jnp.where(adapter_of_lane == labels[:, 0:1], projected, 0.0)
    folded = sum(chosen[:, i : i + lanes] for i in range(0, width, lanes))
    own_both = folded + pltpu.roll(folded, rank, 1)
    sums[...] = jnp.where(low, own_both, pltpu.roll(projected[:, :lanes], rank, 1))

    half, quarter, share = total // 2, total // 4, total // (4 * Z)
    half_at = c * half
    quarter_at = half_at + y * quarter
    share_at = quarter_at + z * share

    def span(start, size):
        return pl.ds(pl.multiple_of(start, 8), size)

    def part(src, dst, there, slot_in, slot_out):
        return pltpu.make_async_remote_copy(
            src_ref=src,
            dst_ref=dst,
            send_sem=part_send.at[slot_out],
            recv_sem=part_recv.at[slot_in],
            device_id={"row": there},
            device_id_type=pl.DeviceIdType.MESH,
        )

    def halves():
        src = sums.at[span((1 - c) * half, half)]
        return part(src, half_in, target[TWIN], 0, 0)

    def quarters():
        src = sums.at[span(half_at + (1 - y) * quarter, quarter)]
        return part(src, quarter_in, target[ACROSS], 1, 1)

    def shares(zz, mine):
        src = sums.at[span(quarter_at + zz * share, share)]
        return part(src, share_in.at[z], blk(zz, y, c), 4 + jnp.where(mine, z, zz), 4 + zz)

    def spread_z(zz, mine):
        rows = span(share_at, share)
        slot = 4 + Z + jnp.where(mine, z, zz)
        return part(totals.at[rows], totals.at[rows], blk(zz, y, c), slot, 4 + Z + zz)

    def spread_y():
        rows = span(quarter_at, quarter)
        return part(totals.at[rows], totals.at[rows], target[ACROSS], 2, 2)

    def spread_c():
        rows = span(half_at, half)
        return part(totals.at[rows], totals.at[rows], target[TWIN], 3, 3)

    def other_planes(f):
        @pl.loop(0, Z)
        def _(zz):
            @pl.when(zz != z)
            def _():
                f(zz)

    halves().start()

    def phase_quarter():
        halves().wait_recv()
        sums[span(half_at, half), :] += half_in[...]
        quarters().start()

    def phase_share():
        quarters().wait_recv()
        sums[span(quarter_at, quarter), :] += quarter_in[...]
        other_planes(lambda zz: shares(zz, True).start())

    def phase_total():
        other_planes(lambda zz: shares(zz, False).wait_recv())
        rows = span(share_at, share)
        totals[rows, :] = sums[rows, :]

        def add(zz):
            totals[rows, :] += share_in[zz]

        other_planes(add)
        other_planes(lambda zz: spread_z(zz, True).start())

    def phase_across():
        other_planes(lambda zz: spread_z(zz, False).wait_recv())
        spread_y().start()

    def phase_twin():
        spread_y().wait_recv()
        spread_c().start()

    def phase_update():
        spread_c().wait_recv()
        summed = totals[...]
        swapped = pltpu.roll(summed, rank, 1)
        label = labels[:, 0:1]
        kept = label != 0.0
        own = jnp.where(low, summed, swapped)
        resident = jnp.where(low, swapped, summed)
        own_wide = jnp.concatenate([own] * (width // lanes), axis=1)
        operand = jnp.where((adapter_of_lane == label) & kept, own_wide, 0.0).astype(jnp.bfloat16)
        rounded = resident.astype(jnp.bfloat16).astype(jnp.float32)
        remaining = jnp.where(kept, resident - rounded, resident)
        upper = remaining.astype(jnp.bfloat16).astype(jnp.float32)
        pair = jnp.where(low, upper, remaining - upper).astype(jnp.bfloat16)
        resident_weight = jnp.concatenate([b_ref[0:rank, :], b_ref[0:rank, :]], axis=0)
        acc[...] += jnp.dot(
            operand, b_ref[...], preferred_element_type=jnp.float32
        ) + jnp.dot(pair, resident_weight, preferred_element_type=jnp.float32)

    phases = (
        (1, 6, phase_quarter),
        (2, 2, phase_share),
        (2, 6, phase_total),
        (3, 2, phase_across),
        (3, 6, phase_twin),
        (4, 3, phase_update),
    )

    def from_left(k, j, across):
        arrived(k, j)
        go_right(k, j)
        if across:
            remote(k, j, ACROSS).start()
        remote(k, j, TWIN).start()

    def from_right(k, j, across):
        arrived(k, j)
        go_left(k, j)
        if across:
            remote(k, j, ACROSS).start()
        remote(k, j, TWIN).start()

    @pl.loop(1, Z + 3)
    def _(d):
        zl, zr = z - d, z + d
        yl, yr = z - (d - 2), z + (d - 2)

        @pl.when(d == 1)
        def _():
            k = blk(z, 1 - y, c)
            arrived(k, NA)
            go_right(k, NA)
            go_left(k, NA)
            remote(k, NA, TWIN).start()

        @pl.loop(0, 8)
        def _(j):
            @pl.when(j < NA)
            def _():
                @pl.when(zl >= 0)
                def _():
                    from_left(blk(zl, y, c), j, True)

                @pl.when(zr < Z)
                def _():
                    from_right(blk(zr, y, c), j, True)

                @pl.when((yl >= 0) & (d > 1))
                def _():
                    k = blk(yl, 1 - y, c)
                    arrived(k, j)
                    remote(k, j, TWIN).start()

                @pl.when((yr < Z) & (d > 2))
                def _():
                    k = blk(yr, 1 - y, c)
                    arrived(k, j)
                    remote(k, j, TWIN).start()

            @pl.when((j == NA) | (j == NA + 1))
            def _():
                yy = jnp.where(j == NA, y, 1 - y)

                @pl.when(zl >= 0)
                def _():
                    from_left(blk(zl, yy, c), NA, False)

                @pl.when(zr < Z)
                def _():
                    from_right(blk(zr, yy, c), NA, False)

            for at_d, at_j, phase in phases:
                pl.when((d == at_d) & (j == at_j))(phase)

            e = d - 1
            twin, kind = j // 4, lax.rem(j, 4)
            crossed, up = kind // 2, lax.rem(kind, 2)
            dist = e - 2 * crossed
            zz = jnp.where(up == 1, z + dist, z - dist)
            valid = (dist >= 0) & (zz >= 0) & (zz < Z) & ((up == 0) | (dist > 0))

            @pl.when(valid)
            def _():
                k = blk(zz, jnp.where(crossed == 1, 1 - y, y), jnp.where(twin == 1, 1 - c, c))

                @pl.when(twin == 1)
                def _():
                    @pl.loop(0, NA + 1)
                    def _(i):
                        arrived(k, i)

                weight(k).wait()
                acc[...] += lax.dot_general(
                    hbuf[k], wbuf[k], CONTRACT, preferred_element_type=jnp.float32
                )

    out_ref[...] = acc[...].astype(out_ref.dtype)

    @pl.loop(0, Z)
    def _(zz):
        @pl.loop(0, 2)
        def _(yy):
            k = blk(zz, yy, c)

            @pl.loop(0, NA + 1)
            def _(j):
                along = (yy == y) | (j == NA)

                @pl.when(has_right & (zz <= z) & along)
                def _():
                    remote(k, j, RIGHT).wait_send()

                @pl.when(has_left & (zz >= z) & along)
                def _():
                    remote(k, j, LEFT).wait_send()

                @pl.when((yy == y) & ((j < NA) | (zz == z)))
                def _():
                    remote(k, j, ACROSS).wait_send()

                remote(k, j, TWIN).wait_send()

    halves().wait_send()
    quarters().wait_send()
    other_planes(lambda zz: shares(zz, True).wait_send())
    other_planes(lambda zz: spread_z(zz, True).wait_send())
    spread_y().wait_send()
    spread_c().wait_send()


def served(n, rows_in, weight, factor_in, factor_out, adapter_index):
    total, units = rows_in.shape
    features = weight.shape[0]
    width = factor_in.shape[0]
    lanes = 128
    parts = 6
    chunk = total // parts
    Z = n // 4
    vmem = pl.BlockSpec(memory_space=pltpu.VMEM)
    return pl.pallas_call(
        functools.partial(served_kernel, Z, parts - 1, chunk),
        out_shape=jax.ShapeDtypeStruct((total, features), jnp.bfloat16),
        in_specs=[pl.BlockSpec(memory_space=pl.ANY)] * 2 + [vmem] * 3,
        out_specs=vmem,
        scratch_shapes=[
            pltpu.VMEM((n, total, units), jnp.bfloat16),
            pltpu.VMEM((n, features, units), jnp.bfloat16),
            pltpu.VMEM((total, features), jnp.float32),
            pltpu.VMEM((total, lanes), jnp.float32),
            pltpu.VMEM((total, lanes), jnp.float32),
            pltpu.VMEM((total, lanes), jnp.float32),
            pltpu.VMEM((total // 2, lanes), jnp.float32),
            pltpu.VMEM((total // 4, lanes), jnp.float32),
            pltpu.VMEM((Z, total // n, lanes), jnp.float32),
            pltpu.SemaphoreType.DMA,
            pltpu.SemaphoreType.DMA((n,)),
            pltpu.SemaphoreType.DMA((n, parts)),
            pltpu.SemaphoreType.DMA((4, n // 2, parts)),
            pltpu.SemaphoreType.DMA((4 + 2 * Z,)),
            pltpu.SemaphoreType.DMA((4 + 2 * Z,)),
        ],
        compiler_params=pltpu.CompilerParams(
            collective_id=0, has_side_effects=True, vmem_limit_bytes=62 * 2**20
        ),
        cost_estimate=pl.CostEstimate(
            flops=2 * total * units * (n * features + width),
            bytes_accessed=2 * n * units * (features + total),
            transcendentals=0,
        ),
    )(rows_in, weight, factor_in, factor_out, adapter_index)


def local(
    n,
    gated_hidden_rows,
    down_base_weight,
    adapter_input_factor,
    adapter_output_weight,
    request_adapter_index,
):
    steps, requests, device_units = gated_hidden_rows.shape
    request_count = adapter_input_factor.shape[0]
    rank_index = adapter_input_factor.shape[1]
    total = steps * requests
    flattened_rows = gated_hidden_rows.reshape(total, device_units)
    fits = 2 * n * device_units * (total + down_base_weight.shape[0]) <= 54 * 2**20
    whole_tiles = device_units % 128 == 0 and total % 96 == 0 and total % (8 * n) == 0
    if n % 16 == 0 and whole_tiles and rank_index == 64 and request_count % 2 == 0 and fits:
        return served(
            n,
            flattened_rows,
            down_base_weight,
            adapter_input_factor.reshape(request_count * rank_index, device_units),
            adapter_output_weight.reshape(request_count * rank_index, down_base_weight.shape[0]),
            request_adapter_index,
        ).reshape(steps, requests, down_base_weight.shape[0])
    adapter_labels = request_adapter_index.reshape(total)
    project_rows = jnp.dot(
        flattened_rows,
        adapter_input_factor.reshape(request_count * rank_index, device_units).T,
        preferred_element_type=jnp.float32,
    )
    summand = select_both(project_rows, adapter_labels, request_count, rank_index)
    summed = lax.psum(summand, "row")
    keep = (adapter_labels != 0).astype(jnp.float32)[:, None]
    shrunk_rows = (summed * keep).astype(jnp.bfloat16)
    resident_sum = summed[:, rank_index:]
    highest = lax.Precision.HIGHEST
    base = lax.dot_general(
        lax.all_gather(flattened_rows, "row", axis=1, tiled=True),
        down_base_weight,
        CONTRACT,
        preferred_element_type=jnp.float32,
    )
    base = base + jnp.dot(
        resident_sum, adapter_output_weight[0].astype(jnp.float32), precision=highest
    )
    adapter_update = expand_factor(shrunk_rows, adapter_labels, adapter_output_weight)
    return (base + adapter_update).astype(jnp.bfloat16).reshape(steps, requests, base.shape[1])


def solution(mesh):
    placed = (
        P(None, "groups", "row"),
        P("row", None),
        P(None, None, "row"),
        P(None, None, "row"),
        P(None, "groups"),
    )
    return jax.shard_map(
        functools.partial(local, mesh.shape["row"]),
        mesh=mesh,
        in_specs=placed,
        out_specs=P(None, "groups", "row"),
        check_vma=False,
    )
```

```python
import functools

import jax
import jax.numpy as jnp
from jax import lax
from jax.experimental import pallas as pl
from jax.experimental.pallas import tpu as pltpu
from jax.sharding import PartitionSpec as P

CONTRACT = (((1,), (1,)), ((), ()))


def select_both(project_rows, adapter_labels, request_count, rank_index):
    choose = (
        adapter_labels[:, None] == jnp.arange(request_count, dtype=jnp.int32)[None, :]
    ).astype(jnp.float32)
    total = project_rows.shape[0]
    own = jnp.sum(
        project_rows.reshape(total, request_count, rank_index) * choose[:, :, None], axis=1
    )
    return jnp.concatenate([own, project_rows[:, :rank_index]], axis=1)


def expand_factor(shrunk_rows, adapter_labels, adapter_output_weight):
    request_count = adapter_output_weight.shape[0]
    rank_index = adapter_output_weight.shape[1]
    total = shrunk_rows.shape[0]
    choose = (
        adapter_labels[:, None] == jnp.arange(request_count, dtype=jnp.int32)[None, :]
    ).astype(jnp.float32)
    spread = (choose[:, :, None] * shrunk_rows[:, None, :rank_index].astype(jnp.float32)).reshape(
        total, request_count * rank_index
    )
    operand = jnp.concatenate([spread.astype(jnp.bfloat16), shrunk_rows[:, rank_index:]], axis=1)
    stacked_weights = jnp.concatenate(
        [
            adapter_output_weight.reshape(
                request_count * rank_index, adapter_output_weight.shape[2]
            ),
            -adapter_output_weight[0],
        ],
        axis=0,
    )
    return jnp.dot(operand, stacked_weights, preferred_element_type=jnp.float32)


def served_kernel(
    Z,
    NA,
    CH,
    x_ref,
    w_ref,
    a_ref,
    b_ref,
    label_ref,
    out_ref,
    hbuf,
    wbuf,
    acc,
    labels,
    sums,
    totals,
    half_in,
    quarter_in,
    share_in,
    a_buf,
    b_buf,
    xsem,
    asem,
    bsem,
    wsem,
    rsem,
    ssem,
    part_recv,
    part_send,
):
    n = 4 * Z
    me = lax.axis_index("row")
    c = lax.rem(me, 2)
    y = lax.rem(me // 2, 2)
    z = me // 4
    units = x_ref.shape[1]
    RIGHT, LEFT, ACROSS, TWIN = 0, 1, 2, 3

    def blk(zz, yy, cc):
        return (zz * 2 + yy) * 2 + cc

    target = (
        blk(jnp.minimum(z + 1, Z - 1), y, c),
        blk(jnp.maximum(z - 1, 0), y, c),
        blk(z, 1 - y, c),
        blk(z, y, 1 - c),
    )
    has_right, has_left = z < Z - 1, z > 0

    def remote(k, j, way):
        rows = pl.ds(pl.multiple_of(j * CH, CH), CH)
        return pltpu.make_async_remote_copy(
            src_ref=hbuf.at[k, rows],
            dst_ref=hbuf.at[k, rows],
            send_sem=ssem.at[way, k // 2, j],
            recv_sem=rsem.at[k, j],
            device_id={"row": target[way]},
            device_id_type=pl.DeviceIdType.MESH,
        )

    def arrived(k, j):
        remote(k, j, TWIN).wait_recv()

    def weight(k):
        cols = pl.ds(pl.multiple_of(k * units, 128), units)
        return pltpu.make_async_copy(w_ref.at[:, cols], wbuf.at[k], wsem.at[k])

    own = pltpu.make_async_copy(x_ref, hbuf.at[me], xsem)
    own.start()
    factor_in = pltpu.make_async_copy(a_ref, a_buf, asem)
    factor_in.start()
    factor_out = pltpu.make_async_copy(b_ref, b_buf, bsem)
    factor_out.start()

    barrier = pltpu.get_barrier_semaphore()

    def greet(dev):
        pl.semaphore_signal(
            barrier, inc=1, device_id={"row": dev}, device_id_type=pl.DeviceIdType.MESH
        )

    greet(target[ACROSS])
    greet(target[TWIN])

    @pl.loop(0, Z)
    def _(zz):
        @pl.when(zz != z)
        def _():
            greet(blk(zz, y, c))

    pl.semaphore_wait(barrier, Z + 1)
    own.wait()

    def go_right(k, j):
        @pl.when(has_right)
        def _():
            remote(k, j, RIGHT).start()

    def go_left(k, j):
        @pl.when(has_left)
        def _():
            remote(k, j, LEFT).start()

    def along_z(j):
        go_right(me, j)
        go_left(me, j)

    remote(me, NA, ACROSS).start()
    along_z(0)
    along_z(1)

    @pl.loop(0, NA + 1)
    def _(j):
        remote(me, j, TWIN).start()

    @pl.loop(0, n)
    def _(k):
        weight(k).start()

    total, lanes = sums.shape
    rank = lanes // 2
    steps, requests = label_ref.shape
    same = lax.broadcasted_iota(jnp.int32, (requests, requests), 0) == (
        lax.broadcasted_iota(jnp.int32, (requests, requests), 1)
    )
    for s in range(steps):
        row = label_ref[s : s + 1, :].astype(jnp.float32)
        column = jnp.sum(jnp.where(same, row, 0.0), axis=1, keepdims=True)
        labels[s * requests : (s + 1) * requests, :] = jnp.broadcast_to(column, (requests, lanes))

    width = a_ref.shape[0]
    adapter_of_lane = (lax.broadcasted_iota(jnp.int32, (1, width), 1) // rank).astype(jnp.float32)
    low = lax.broadcasted_iota(jnp.int32, (1, lanes), 1) < rank
    factor_in.wait()
    projected = lax.dot_general(
        hbuf[me], a_buf[...], CONTRACT, preferred_element_type=jnp.float32
    )
    chosen = jnp.where(adapter_of_lane == labels[:, 0:1], projected, 0.0)
    folded = sum(chosen[:, i : i + lanes] for i in range(0, width, lanes))
    own_both = folded + pltpu.roll(folded, rank, 1)
    sums[...] = jnp.where(low, own_both, pltpu.roll(projected[:, :lanes], rank, 1))

    half, quarter, share = total // 2, total // 4, total // (4 * Z)
    half_at = c * half
    quarter_at = half_at + y * quarter
    share_at = quarter_at + z * share

    def span(start, size):
        return pl.ds(pl.multiple_of(start, 8), size)

    def part(src, dst, there, slot_in, slot_out):
        return pltpu.make_async_remote_copy(
            src_ref=src,
            dst_ref=dst,
            send_sem=part_send.at[slot_out],
            recv_sem=part_recv.at[slot_in],
            device_id={"row": there},
            device_id_type=pl.DeviceIdType.MESH,
        )

    def halves():
        src = sums.at[span((1 - c) * half, half)]
        return part(src, half_in, target[TWIN], 0, 0)

    def quarters():
        src = sums.at[span(half_at + (1 - y) * quarter, quarter)]
        return part(src, quarter_in, target[ACROSS], 1, 1)

    def shares(zz, mine):
        src = sums.at[span(quarter_at + zz * share, share)]
        return part(src, share_in.at[z], blk(zz, y, c), 4 + jnp.where(mine, z, zz), 4 + zz)

    def spread_z(zz, mine):
        rows = span(share_at, share)
        slot = 4 + Z + jnp.where(mine, z, zz)
        return part(totals.at[rows], totals.at[rows], blk(zz, y, c), slot, 4 + Z + zz)

    def spread_y():
        rows = span(quarter_at, quarter)
        return part(totals.at[rows], totals.at[rows], target[ACROSS], 2, 2)

    def spread_c():
        rows = span(half_at, half)
        return part(totals.at[rows], totals.at[rows], target[TWIN], 3, 3)

    def other_planes(f):
        @pl.loop(0, Z)
        def _(zz):
            @pl.when(zz != z)
            def _():
                f(zz)

    halves().start()
    acc[...] = jnp.zeros_like(acc)

    def phase_quarter():
        halves().wait_recv()
        sums[span(half_at, half), :] += half_in[...]
        quarters().start()

    def phase_share():
        quarters().wait_recv()
        sums[span(quarter_at, quarter), :] += quarter_in[...]
        other_planes(lambda zz: shares(zz, True).start())

    def phase_total():
        other_planes(lambda zz: shares(zz, False).wait_recv())
        rows = span(share_at, share)
        totals[rows, :] = sums[rows, :]

        def add(zz):
            totals[rows, :] += share_in[zz]

        other_planes(add)
        other_planes(lambda zz: spread_z(zz, True).start())

    def phase_across():
        other_planes(lambda zz: spread_z(zz, False).wait_recv())
        spread_y().start()

    def phase_twin():
        spread_y().wait_recv()
        spread_c().start()

    def phase_update():
        spread_c().wait_recv()
        factor_out.wait()
        summed = totals[...]
        swapped = pltpu.roll(summed, rank, 1)
        label = labels[:, 0:1]
        kept = label != 0.0
        own = jnp.where(low, summed, swapped)
        resident = jnp.where(low, swapped, summed)
        own_wide = jnp.concatenate([own] * (width // lanes), axis=1)
        operand = jnp.where((adapter_of_lane == label) & kept, own_wide, 0.0).astype(jnp.bfloat16)
        rounded = resident.astype(jnp.bfloat16).astype(jnp.float32)
        remaining = jnp.where(kept, resident - rounded, resident)
        upper = remaining.astype(jnp.bfloat16).astype(jnp.float32)
        pair = jnp.where(low, upper, remaining - upper).astype(jnp.bfloat16)
        resident_weight = jnp.concatenate([b_buf[0:rank, :], b_buf[0:rank, :]], axis=0)
        acc[...] += jnp.dot(
            operand, b_buf[...], preferred_element_type=jnp.float32
        ) + jnp.dot(pair, resident_weight, preferred_element_type=jnp.float32)

    phase_quarter()
    remote(me, 0, ACROSS).start()
    along_z(2)
    phase_share()
    remote(me, 1, ACROSS).start()
    remote(me, 2, ACROSS).start()
    along_z(3)
    phase_total()

    @pl.loop(3, NA)
    def _(j):
        remote(me, j, ACROSS).start()

    @pl.loop(4, NA + 1)
    def _(j):
        along_z(j)

    phases = ((1, 1, phase_across), (1, 7, phase_twin), (2, 3, phase_update))

    def from_left(k, j, across):
        arrived(k, j)
        go_right(k, j)
        if across:
            remote(k, j, ACROSS).start()
        remote(k, j, TWIN).start()

    def from_right(k, j, across):
        arrived(k, j)
        go_left(k, j)
        if across:
            remote(k, j, ACROSS).start()
        remote(k, j, TWIN).start()

    @pl.loop(1, Z + 3)
    def _(d):
        zl, zr = z - d, z + d
        yl, yr = z - (d - 2), z + (d - 2)

        @pl.when(d == 1)
        def _():
            k = blk(z, 1 - y, c)
            arrived(k, NA)
            go_right(k, NA)
            go_left(k, NA)
            remote(k, NA, TWIN).start()

        @pl.loop(0, 8)
        def _(j):
            @pl.when(j < NA)
            def _():
                @pl.when(zl >= 0)
                def _():
                    from_left(blk(zl, y, c), j, True)

                @pl.when(zr < Z)
                def _():
                    from_right(blk(zr, y, c), j, True)

                @pl.when((yl >= 0) & (d > 1))
                def _():
                    k = blk(yl, 1 - y, c)
                    arrived(k, j)
                    remote(k, j, TWIN).start()

                @pl.when((yr < Z) & (d > 2))
                def _():
                    k = blk(yr, 1 - y, c)
                    arrived(k, j)
                    remote(k, j, TWIN).start()

            @pl.when((j == NA) | (j == NA + 1))
            def _():
                yy = jnp.where(j == NA, y, 1 - y)

                @pl.when(zl >= 0)
                def _():
                    from_left(blk(zl, yy, c), NA, False)

                @pl.when(zr < Z)
                def _():
                    from_right(blk(zr, yy, c), NA, False)

            for at_d, at_j, phase in phases:
                pl.when((d == at_d) & (j == at_j))(phase)

            e = d - 1
            twin, kind = j // 4, lax.rem(j, 4)
            crossed, up = kind // 2, lax.rem(kind, 2)
            dist = e - 2 * crossed
            zz = jnp.where(up == 1, z + dist, z - dist)
            valid = (dist >= 0) & (zz >= 0) & (zz < Z) & ((up == 0) | (dist > 0))

            @pl.when(valid)
            def _():
                k = blk(zz, jnp.where(crossed == 1, 1 - y, y), jnp.where(twin == 1, 1 - c, c))

                @pl.when(twin == 1)
                def _():
                    @pl.loop(0, NA + 1)
                    def _(i):
                        arrived(k, i)

                weight(k).wait()
                acc[...] += lax.dot_general(
                    hbuf[k], wbuf[k], CONTRACT, preferred_element_type=jnp.float32
                )

    out_ref[...] = acc[...].astype(out_ref.dtype)

    @pl.loop(0, Z)
    def _(zz):
        @pl.loop(0, 2)
        def _(yy):
            k = blk(zz, yy, c)

            @pl.loop(0, NA + 1)
            def _(j):
                along = (yy == y) | (j == NA)

                @pl.when(has_right & (zz <= z) & along)
                def _():
                    remote(k, j, RIGHT).wait_send()

                @pl.when(has_left & (zz >= z) & along)
                def _():
                    remote(k, j, LEFT).wait_send()

                @pl.when((yy == y) & ((j < NA) | (zz == z)))
                def _():
                    remote(k, j, ACROSS).wait_send()

                remote(k, j, TWIN).wait_send()

    halves().wait_send()
    quarters().wait_send()
    other_planes(lambda zz: shares(zz, True).wait_send())
    other_planes(lambda zz: spread_z(zz, True).wait_send())
    spread_y().wait_send()
    spread_c().wait_send()


def served(n, rows_in, weight, factor_in, factor_out, adapter_index):
    total, units = rows_in.shape
    features = weight.shape[0]
    width = factor_in.shape[0]
    lanes = 128
    parts = 6
    chunk = total // parts
    Z = n // 4
    vmem = pl.BlockSpec(memory_space=pltpu.VMEM)
    return pl.pallas_call(
        functools.partial(served_kernel, Z, parts - 1, chunk),
        out_shape=jax.ShapeDtypeStruct((total, features), jnp.bfloat16),
        in_specs=[pl.BlockSpec(memory_space=pl.ANY)] * 4 + [vmem],
        out_specs=vmem,
        scratch_shapes=[
            pltpu.VMEM((n, total, units), jnp.bfloat16),
            pltpu.VMEM((n, features, units), jnp.bfloat16),
            pltpu.VMEM((total, features), jnp.float32),
            pltpu.VMEM((total, lanes), jnp.float32),
            pltpu.VMEM((total, lanes), jnp.float32),
            pltpu.VMEM((total, lanes), jnp.float32),
            pltpu.VMEM((total // 2, lanes), jnp.float32),
            pltpu.VMEM((total // 4, lanes), jnp.float32),
            pltpu.VMEM((Z, total // n, lanes), jnp.float32),
            pltpu.VMEM((width, units), jnp.bfloat16),
            pltpu.VMEM((width, features), jnp.bfloat16),
            pltpu.SemaphoreType.DMA,
            pltpu.SemaphoreType.DMA,
            pltpu.SemaphoreType.DMA,
            pltpu.SemaphoreType.DMA((n,)),
            pltpu.SemaphoreType.DMA((n, parts)),
            pltpu.SemaphoreType.DMA((4, n // 2, parts)),
            pltpu.SemaphoreType.DMA((4 + 2 * Z,)),
            pltpu.SemaphoreType.DMA((4 + 2 * Z,)),
        ],
        compiler_params=pltpu.CompilerParams(
            collective_id=0, has_side_effects=True, vmem_limit_bytes=62 * 2**20
        ),
        cost_estimate=pl.CostEstimate(
            flops=2 * total * units * (n * features + width),
            bytes_accessed=2 * n * units * (features + total),
            transcendentals=0,
        ),
    )(rows_in, weight, factor_in, factor_out, adapter_index)


def local(
    n,
    gated_hidden_rows,
    down_base_weight,
    adapter_input_factor,
    adapter_output_weight,
    request_adapter_index,
):
    steps, requests, device_units = gated_hidden_rows.shape
    request_count = adapter_input_factor.shape[0]
    rank_index = adapter_input_factor.shape[1]
    total = steps * requests
    flattened_rows = gated_hidden_rows.reshape(total, device_units)
    fits = 2 * n * device_units * (total + down_base_weight.shape[0]) <= 54 * 2**20
    whole_tiles = device_units % 128 == 0 and total % 96 == 0 and total % (8 * n) == 0
    if n % 16 == 0 and whole_tiles and rank_index == 64 and request_count % 2 == 0 and fits:
        return served(
            n,
            flattened_rows,
            down_base_weight,
            adapter_input_factor.reshape(request_count * rank_index, device_units),
            adapter_output_weight.reshape(request_count * rank_index, down_base_weight.shape[0]),
            request_adapter_index,
        ).reshape(steps, requests, down_base_weight.shape[0])
    adapter_labels = request_adapter_index.reshape(total)
    project_rows = jnp.dot(
        flattened_rows,
        adapter_input_factor.reshape(request_count * rank_index, device_units).T,
        preferred_element_type=jnp.float32,
    )
    summand = select_both(project_rows, adapter_labels, request_count, rank_index)
    summed = lax.psum(summand, "row")
    keep = (adapter_labels != 0).astype(jnp.float32)[:, None]
    shrunk_rows = (summed * keep).astype(jnp.bfloat16)
    resident_sum = summed[:, rank_index:]
    highest = lax.Precision.HIGHEST
    base = lax.dot_general(
        lax.all_gather(flattened_rows, "row", axis=1, tiled=True),
        down_base_weight,
        CONTRACT,
        preferred_element_type=jnp.float32,
    )
    base = base + jnp.dot(
        resident_sum, adapter_output_weight[0].astype(jnp.float32), precision=highest
    )
    adapter_update = expand_factor(shrunk_rows, adapter_labels, adapter_output_weight)
    return (base + adapter_update).astype(jnp.bfloat16).reshape(steps, requests, base.shape[1])


def solution(mesh):
    placed = (
        P(None, "groups", "row"),
        P("row", None),
        P(None, None, "row"),
        P(None, None, "row"),
        P(None, "groups"),
    )
    return jax.shard_map(
        functools.partial(local, mesh.shape["row"]),
        mesh=mesh,
        in_specs=placed,
        out_specs=P(None, "groups", "row"),
        check_vma=False,
    )
```

```python
import functools

import jax
import jax.numpy as jnp
from jax import lax
from jax.experimental import pallas as pl
from jax.experimental.pallas import tpu as pltpu
from jax.sharding import PartitionSpec as P

CONTRACT = (((1,), (1,)), ((), ()))


def select_both(project_rows, adapter_labels, request_count, rank_index):
    choose = (
        adapter_labels[:, None] == jnp.arange(request_count, dtype=jnp.int32)[None, :]
    ).astype(jnp.float32)
    total = project_rows.shape[0]
    own = jnp.sum(
        project_rows.reshape(total, request_count, rank_index) * choose[:, :, None], axis=1
    )
    return jnp.concatenate([own, project_rows[:, :rank_index]], axis=1)


def expand_factor(shrunk_rows, adapter_labels, adapter_output_weight):
    request_count = adapter_output_weight.shape[0]
    rank_index = adapter_output_weight.shape[1]
    total = shrunk_rows.shape[0]
    choose = (
        adapter_labels[:, None] == jnp.arange(request_count, dtype=jnp.int32)[None, :]
    ).astype(jnp.float32)
    spread = (choose[:, :, None] * shrunk_rows[:, None, :rank_index].astype(jnp.float32)).reshape(
        total, request_count * rank_index
    )
    operand = jnp.concatenate([spread.astype(jnp.bfloat16), shrunk_rows[:, rank_index:]], axis=1)
    stacked_weights = jnp.concatenate(
        [
            adapter_output_weight.reshape(
                request_count * rank_index, adapter_output_weight.shape[2]
            ),
            -adapter_output_weight[0],
        ],
        axis=0,
    )
    return jnp.dot(operand, stacked_weights, preferred_element_type=jnp.float32)


def served_kernel(
    Z,
    NA,
    CH,
    x_ref,
    w_ref,
    a_ref,
    b_ref,
    label_ref,
    out_ref,
    hbuf,
    wbuf,
    acc,
    labels,
    sums,
    totals,
    half_in,
    quarter_in,
    share_in,
    a_buf,
    b_buf,
    xsem,
    asem,
    bsem,
    wsem,
    rsem,
    ssem,
    part_recv,
    part_send,
):
    n = 4 * Z
    me = lax.axis_index("row")
    c = lax.rem(me, 2)
    y = lax.rem(me // 2, 2)
    z = me // 4
    units = x_ref.shape[1]
    RIGHT, LEFT, ACROSS, TWIN = 0, 1, 2, 3

    def blk(zz, yy, cc):
        return (zz * 2 + yy) * 2 + cc

    target = (
        blk(jnp.minimum(z + 1, Z - 1), y, c),
        blk(jnp.maximum(z - 1, 0), y, c),
        blk(z, 1 - y, c),
        blk(z, y, 1 - c),
    )
    has_right, has_left = z < Z - 1, z > 0

    def remote(k, j, way):
        rows = pl.ds(pl.multiple_of(j * CH, CH), CH)
        return pltpu.make_async_remote_copy(
            src_ref=hbuf.at[k, rows],
            dst_ref=hbuf.at[k, rows],
            send_sem=ssem.at[way, k // 2, j],
            recv_sem=rsem.at[k, j],
            device_id={"row": target[way]},
            device_id_type=pl.DeviceIdType.MESH,
        )

    def arrived(k, j):
        remote(k, j, TWIN).wait_recv()

    def weight(k):
        cols = pl.ds(pl.multiple_of(k * units, 128), units)
        return pltpu.make_async_copy(w_ref.at[:, cols], wbuf.at[k], wsem.at[k])

    own = pltpu.make_async_copy(x_ref, hbuf.at[me], xsem)
    own.start()
    factor_in = pltpu.make_async_copy(a_ref, a_buf, asem)
    factor_in.start()
    factor_out = pltpu.make_async_copy(b_ref, b_buf, bsem)
    factor_out.start()

    barrier = pltpu.get_barrier_semaphore()

    def greet(dev):
        pl.semaphore_signal(
            barrier, inc=1, device_id={"row": dev}, device_id_type=pl.DeviceIdType.MESH
        )

    greet(target[ACROSS])
    greet(target[TWIN])

    @pl.loop(0, Z)
    def _(zz):
        @pl.when(zz != z)
        def _():
            greet(blk(zz, y, c))

    pl.semaphore_wait(barrier, Z + 1)
    own.wait()

    def go_right(k, j):
        @pl.when(has_right)
        def _():
            remote(k, j, RIGHT).start()

    def go_left(k, j):
        @pl.when(has_left)
        def _():
            remote(k, j, LEFT).start()

    def along_z(j):
        go_right(me, j)
        go_left(me, j)

    remote(me, NA, ACROSS).start()
    along_z(0)
    along_z(1)

    @pl.loop(0, NA + 1)
    def _(j):
        remote(me, j, TWIN).start()

    @pl.loop(0, n)
    def _(k):
        weight(k).start()

    total, lanes = sums.shape
    rank = lanes // 2
    steps, requests = label_ref.shape
    same = lax.broadcasted_iota(jnp.int32, (requests, requests), 0) == (
        lax.broadcasted_iota(jnp.int32, (requests, requests), 1)
    )
    for s in range(steps):
        row = label_ref[s : s + 1, :].astype(jnp.float32)
        column = jnp.sum(jnp.where(same, row, 0.0), axis=1, keepdims=True)
        labels[s * requests : (s + 1) * requests, :] = jnp.broadcast_to(column, (requests, lanes))

    width = a_ref.shape[0]
    adapter_of_lane = (lax.broadcasted_iota(jnp.int32, (1, width), 1) // rank).astype(jnp.float32)
    low = lax.broadcasted_iota(jnp.int32, (1, lanes), 1) < rank
    factor_in.wait()
    projected = lax.dot_general(
        hbuf[me], a_buf[...], CONTRACT, preferred_element_type=jnp.float32
    )
    chosen = jnp.where(adapter_of_lane == labels[:, 0:1], projected, 0.0)
    folded = sum(chosen[:, i : i + lanes] for i in range(0, width, lanes))
    own_both = folded + pltpu.roll(folded, rank, 1)
    sums[...] = jnp.where(low, own_both, pltpu.roll(projected[:, :lanes], rank, 1))

    half, quarter, share = total // 2, total // 4, total // (4 * Z)
    half_at = c * half
    quarter_at = half_at + y * quarter
    share_at = quarter_at + z * share

    def span(start, size):
        return pl.ds(pl.multiple_of(start, 8), size)

    def part(src, dst, there, slot_in, slot_out):
        return pltpu.make_async_remote_copy(
            src_ref=src,
            dst_ref=dst,
            send_sem=part_send.at[slot_out],
            recv_sem=part_recv.at[slot_in],
            device_id={"row": there},
            device_id_type=pl.DeviceIdType.MESH,
        )

    def halves():
        src = sums.at[span((1 - c) * half, half)]
        return part(src, half_in, target[TWIN], 0, 0)

    def quarters():
        src = sums.at[span(half_at + (1 - y) * quarter, quarter)]
        return part(src, quarter_in, target[ACROSS], 1, 1)

    def shares(zz, mine):
        src = sums.at[span(quarter_at + zz * share, share)]
        return part(src, share_in.at[z], blk(zz, y, c), 4 + jnp.where(mine, z, zz), 4 + zz)

    def spread_z(zz, mine):
        rows = span(share_at, share)
        slot = 4 + Z + jnp.where(mine, z, zz)
        return part(totals.at[rows], totals.at[rows], blk(zz, y, c), slot, 4 + Z + zz)

    def spread_y():
        rows = span(quarter_at, quarter)
        return part(totals.at[rows], totals.at[rows], target[ACROSS], 2, 2)

    def spread_c():
        rows = span(half_at, half)
        return part(totals.at[rows], totals.at[rows], target[TWIN], 3, 3)

    def other_planes(f):
        @pl.loop(0, Z)
        def _(zz):
            @pl.when(zz != z)
            def _():
                f(zz)

    halves().start()
    acc[...] = jnp.zeros_like(acc)

    def phase_quarter():
        halves().wait_recv()
        sums[span(half_at, half), :] += half_in[...]
        quarters().start()

    def phase_share():
        quarters().wait_recv()
        sums[span(quarter_at, quarter), :] += quarter_in[...]
        other_planes(lambda zz: shares(zz, True).start())

    def phase_total():
        other_planes(lambda zz: shares(zz, False).wait_recv())
        rows = span(share_at, share)
        totals[rows, :] = sums[rows, :]

        def add(zz):
            totals[rows, :] += share_in[zz]

        other_planes(add)
        other_planes(lambda zz: spread_z(zz, True).start())

    def phase_across():
        other_planes(lambda zz: spread_z(zz, False).wait_recv())
        spread_y().start()

    def phase_twin():
        spread_y().wait_recv()
        spread_c().start()

    def phase_update():
        spread_c().wait_recv()
        factor_out.wait()
        summed = totals[...]
        swapped = pltpu.roll(summed, rank, 1)
        label = labels[:, 0:1]
        kept = label != 0.0
        own = jnp.where(low, summed, swapped)
        resident = jnp.where(low, swapped, summed)
        own_wide = jnp.concatenate([own] * (width // lanes), axis=1)
        operand = jnp.where((adapter_of_lane == label) & kept, own_wide, 0.0).astype(jnp.bfloat16)
        rounded = resident.astype(jnp.bfloat16).astype(jnp.float32)
        remaining = jnp.where(kept, resident - rounded, resident)
        upper = remaining.astype(jnp.bfloat16).astype(jnp.float32)
        pair = jnp.where(low, upper, remaining - upper).astype(jnp.bfloat16)
        resident_weight = jnp.concatenate([b_buf[0:rank, :], b_buf[0:rank, :]], axis=0)
        acc[...] += jnp.dot(
            operand, b_buf[...], preferred_element_type=jnp.float32
        ) + jnp.dot(pair, resident_weight, preferred_element_type=jnp.float32)

    phase_quarter()
    remote(me, 0, ACROSS).start()
    along_z(2)
    phase_share()
    remote(me, 1, ACROSS).start()
    remote(me, 2, ACROSS).start()
    along_z(3)
    phase_total()

    @pl.loop(3, NA)
    def _(j):
        remote(me, j, ACROSS).start()

    @pl.loop(4, NA + 1)
    def _(j):
        along_z(j)

    phases = ((1, 1, phase_across), (1, 7, phase_twin), (2, 3, phase_update))

    def from_left(k, j, across):
        arrived(k, j)
        go_right(k, j)
        if across:
            remote(k, j, ACROSS).start()
        remote(k, j, TWIN).start()

    def from_right(k, j, across):
        arrived(k, j)
        go_left(k, j)
        if across:
            remote(k, j, ACROSS).start()
        remote(k, j, TWIN).start()

    @pl.loop(1, Z + 3)
    def _(d):
        zl, zr = z - d, z + d
        yl, yr = z - (d - 2), z + (d - 2)

        @pl.when(d == 1)
        def _():
            k = blk(z, 1 - y, c)
            arrived(k, NA)
            go_right(k, NA)
            go_left(k, NA)
            remote(k, NA, TWIN).start()

        @pl.loop(0, 8)
        def _(j):
            @pl.when(j < NA)
            def _():
                @pl.when(zl >= 0)
                def _():
                    from_left(blk(zl, y, c), j, True)

                @pl.when(zr < Z)
                def _():
                    from_right(blk(zr, y, c), j, True)

                @pl.when((yl >= 0) & (d > 1))
                def _():
                    k = blk(yl, 1 - y, c)
                    arrived(k, j)
                    remote(k, j, TWIN).start()

                @pl.when((yr < Z) & (d > 2))
                def _():
                    k = blk(yr, 1 - y, c)
                    arrived(k, j)
                    remote(k, j, TWIN).start()

            @pl.when((j == NA) | (j == NA + 1))
            def _():
                yy = jnp.where(j == NA, y, 1 - y)

                @pl.when(zl >= 0)
                def _():
                    from_left(blk(zl, yy, c), NA, False)

                @pl.when(zr < Z)
                def _():
                    from_right(blk(zr, yy, c), NA, False)

            for at_d, at_j, phase in phases:
                pl.when((d == at_d) & (j == at_j))(phase)

            e = d - 1
            twin, kind = lax.rem(j, 2), 3 - j // 2
            crossed, up = kind // 2, lax.rem(kind, 2)
            dist = e - 2 * crossed
            zz = jnp.where(up == 1, z + dist, z - dist)
            valid = (dist >= 0) & (zz >= 0) & (zz < Z) & ((up == 0) | (dist > 0))

            @pl.when(valid)
            def _():
                k = blk(zz, jnp.where(crossed == 1, 1 - y, y), jnp.where(twin == 1, 1 - c, c))

                @pl.when(twin == 1)
                def _():
                    @pl.loop(0, NA + 1)
                    def _(i):
                        arrived(k, i)

                weight(k).wait()
                acc[...] += lax.dot_general(
                    hbuf[k], wbuf[k], CONTRACT, preferred_element_type=jnp.float32
                )

    out_ref[...] = acc[...].astype(out_ref.dtype)

    @pl.loop(0, Z)
    def _(zz):
        @pl.loop(0, 2)
        def _(yy):
            k = blk(zz, yy, c)

            @pl.loop(0, NA + 1)
            def _(j):
                along = (yy == y) | (j == NA)

                @pl.when(has_right & (zz <= z) & along)
                def _():
                    remote(k, j, RIGHT).wait_send()

                @pl.when(has_left & (zz >= z) & along)
                def _():
                    remote(k, j, LEFT).wait_send()

                @pl.when((yy == y) & ((j < NA) | (zz == z)))
                def _():
                    remote(k, j, ACROSS).wait_send()

                remote(k, j, TWIN).wait_send()

    halves().wait_send()
    quarters().wait_send()
    other_planes(lambda zz: shares(zz, True).wait_send())
    other_planes(lambda zz: spread_z(zz, True).wait_send())
    spread_y().wait_send()
    spread_c().wait_send()


def served(n, rows_in, weight, factor_in, factor_out, adapter_index):
    total, units = rows_in.shape
    features = weight.shape[0]
    width = factor_in.shape[0]
    lanes = 128
    parts = 6
    chunk = total // parts
    Z = n // 4
    vmem = pl.BlockSpec(memory_space=pltpu.VMEM)
    return pl.pallas_call(
        functools.partial(served_kernel, Z, parts - 1, chunk),
        out_shape=jax.ShapeDtypeStruct((total, features), jnp.bfloat16),
        in_specs=[pl.BlockSpec(memory_space=pl.ANY)] * 4 + [vmem],
        out_specs=vmem,
        scratch_shapes=[
            pltpu.VMEM((n, total, units), jnp.bfloat16),
            pltpu.VMEM((n, features, units), jnp.bfloat16),
            pltpu.VMEM((total, features), jnp.float32),
            pltpu.VMEM((total, lanes), jnp.float32),
            pltpu.VMEM((total, lanes), jnp.float32),
            pltpu.VMEM((total, lanes), jnp.float32),
            pltpu.VMEM((total // 2, lanes), jnp.float32),
            pltpu.VMEM((total // 4, lanes), jnp.float32),
            pltpu.VMEM((Z, total // n, lanes), jnp.float32),
            pltpu.VMEM((width, units), jnp.bfloat16),
            pltpu.VMEM((width, features), jnp.bfloat16),
            pltpu.SemaphoreType.DMA,
            pltpu.SemaphoreType.DMA,
            pltpu.SemaphoreType.DMA,
            pltpu.SemaphoreType.DMA((n,)),
            pltpu.SemaphoreType.DMA((n, parts)),
            pltpu.SemaphoreType.DMA((4, n // 2, parts)),
            pltpu.SemaphoreType.DMA((4 + 2 * Z,)),
            pltpu.SemaphoreType.DMA((4 + 2 * Z,)),
        ],
        compiler_params=pltpu.CompilerParams(
            collective_id=0, has_side_effects=True, vmem_limit_bytes=62 * 2**20
        ),
        cost_estimate=pl.CostEstimate(
            flops=2 * total * units * (n * features + width),
            bytes_accessed=2 * n * units * (features + total),
            transcendentals=0,
        ),
    )(rows_in, weight, factor_in, factor_out, adapter_index)


def local(
    n,
    gated_hidden_rows,
    down_base_weight,
    adapter_input_factor,
    adapter_output_weight,
    request_adapter_index,
):
    steps, requests, device_units = gated_hidden_rows.shape
    request_count = adapter_input_factor.shape[0]
    rank_index = adapter_input_factor.shape[1]
    total = steps * requests
    flattened_rows = gated_hidden_rows.reshape(total, device_units)
    fits = 2 * n * device_units * (total + down_base_weight.shape[0]) <= 54 * 2**20
    whole_tiles = device_units % 128 == 0 and total % 96 == 0 and total % (8 * n) == 0
    if n % 16 == 0 and whole_tiles and rank_index == 64 and request_count % 2 == 0 and fits:
        return served(
            n,
            flattened_rows,
            down_base_weight,
            adapter_input_factor.reshape(request_count * rank_index, device_units),
            adapter_output_weight.reshape(request_count * rank_index, down_base_weight.shape[0]),
            request_adapter_index,
        ).reshape(steps, requests, down_base_weight.shape[0])
    adapter_labels = request_adapter_index.reshape(total)
    project_rows = jnp.dot(
        flattened_rows,
        adapter_input_factor.reshape(request_count * rank_index, device_units).T,
        preferred_element_type=jnp.float32,
    )
    summand = select_both(project_rows, adapter_labels, request_count, rank_index)
    summed = lax.psum(summand, "row")
    keep = (adapter_labels != 0).astype(jnp.float32)[:, None]
    shrunk_rows = (summed * keep).astype(jnp.bfloat16)
    resident_sum = summed[:, rank_index:]
    highest = lax.Precision.HIGHEST
    base = lax.dot_general(
        lax.all_gather(flattened_rows, "row", axis=1, tiled=True),
        down_base_weight,
        CONTRACT,
        preferred_element_type=jnp.float32,
    )
    base = base + jnp.dot(
        resident_sum, adapter_output_weight[0].astype(jnp.float32), precision=highest
    )
    adapter_update = expand_factor(shrunk_rows, adapter_labels, adapter_output_weight)
    return (base + adapter_update).astype(jnp.bfloat16).reshape(steps, requests, base.shape[1])


def solution(mesh):
    placed = (
        P(None, "groups", "row"),
        P("row", None),
        P(None, None, "row"),
        P(None, None, "row"),
        P(None, "groups"),
    )
    return jax.shard_map(
        functools.partial(local, mesh.shape["row"]),
        mesh=mesh,
        in_specs=placed,
        out_specs=P(None, "groups", "row"),
        check_vma=False,
    )
```
